32 devices in a mesh: ctx: 8 (over y, x, core), vocab: 4 (over z).
Axes of the slice: x: 2, y: 2, z: 4, core: 2. Of those that a mesh axis runs over, the one named last changes fastest.
Arguments:
- block_query: bfloat16 [256, 6144], P('ctx', 'vocab'), may hold values from -16 to 16
- block_key: bfloat16 [256, 6144], P('ctx', 'vocab'), may hold values from -16 to 16
- block_value: bfloat16 [256, 6144], P('ctx', 'vocab'), may hold values from -6 to 6
- block_doc: int32 [256], P('ctx'), may hold values from 0 to 1, never falling along the last dimension, each value on 1 to 224 neighbouring positions
- token_query: bfloat16 [1024, 6144], P(('ctx', 'vocab')), may hold values from -16 to 16
- token_key: bfloat16 [1024, 6144], P(('ctx', 'vocab')), may hold values from -16 to 16
- token_value: bfloat16 [1024, 6144], P(('ctx', 'vocab')), may hold values from -600 to 600
- token_state: bfloat16 [1024, 6144], P(('ctx', 'vocab')), may hold values from -6 to 6
- norm_gain: float32 [6144], replicated, may hold values from 0.5 to 1.5
- head_weight: bfloat16 [6144, 32768], P(None, ('ctx', 'vocab')), may hold values from -128 to 128
- targets: int32 [1024], replicated, may hold values from 0 to 32767
Outputs:
- block_context: bfloat16 [256, 6144], P('ctx', 'vocab')
- token_prior: float32 [1024], P(('ctx', 'vocab'))
The draws below stay inside these ranges and needn't reach their ends.
Inputs may be any that keep to these rules, and one draw needn't show every extreme that they name: block_doc never falls along the blocks; no document holds more than 224 blocks.
All inputs are finite; a program needn't handle non-finite values.
Results may differ from the reference program's by a relative error of at most 0.005.
Values may be sent and summed in bfloat16 or wider, within the bound.
A program may use at most 128 MiB of HBM per device.

```python
import math
import jax
import jax.numpy as jnp
import numpy as np
from jax import lax

HEADS = 48
HEAD_DIM = 128
BLOCK_LEN = 4
DOCS = 2
BLK_DEV = 32
WIDTH = 6144
BLOCKS = 256
TOKENS = 1024
VOCAB = 32768


def noise(key, salt, rows):
    return jnp.clip(jax.random.normal(jax.random.fold_in(key, salt), (rows, WIDTH), jnp.float32), -6.0, 6.0)


def draw_block_query(key, part):
    base = noise(key, 11, BLOCKS)
    return base.astype(jnp.bfloat16)


def draw_block_key(key, part):
    base = noise(key, 12, BLOCKS)
    return base.astype(jnp.bfloat16)


def draw_token_query(key, part):
    base = noise(key, 21, TOKENS)
    return base.astype(jnp.bfloat16)


def draw_token_key(key, part):
    base = noise(key, 22, TOKENS)
    return base.astype(jnp.bfloat16)


def draw_token_value(key, part):
    base = noise(key, 23, TOKENS)
    return base.astype(jnp.bfloat16)


def draw_head_weight(key, part):
    column = jnp.arange(VOCAB, dtype=jnp.float32)
    spread = 3.0 / math.sqrt(WIDTH) * (0.6 + 1.2 * column / VOCAB)
    base = jnp.clip(jax.random.normal(jax.random.fold_in(key, 31), (WIDTH, VOCAB), jnp.float32), -6.0, 6.0) * spread[None, :]
    return base.astype(jnp.bfloat16)


def place_ends(values, rng, least, top_value):
    extent = values.shape
    spot = [jax.random.randint(jax.random.fold_in(rng, axis), (), 0, extent[axis]) for axis in range(len(extent))]
    values = values.at[tuple(spot)].set(least)
    longest = extent.index(max(extent))
    spot[longest] = (spot[longest] + 1) % extent[longest]
    return values.at[tuple(spot)].set(top_value)


def shard_levels(rng, shape, pieces, least, top_value):
    gain, own = 1.0, jax.random.fold_in(rng, 6)
    for axis_at, shards_of in pieces:
        heights = jnp.exp(jax.random.uniform(jax.random.fold_in(own, axis_at), (shards_of,), jnp.float32, least / len(pieces), top_value / len(pieces)))
        gain = gain * jnp.repeat(heights, shape[axis_at] // shards_of).reshape([-1 if axis == axis_at else 1 for axis in range(len(shape))])
    return gain


def cumulative_ranks(number_of, skew):
    portions = [(1 << 20) // math.isqrt(rank ** skew) + 1 for rank in range(1, number_of + 1)]
    width = 1 + sum(portions) // (1 << 30)
    return np.cumsum(np.array([max(1, weight // width) for weight in portions]))


def ranked(key, dims, number_of, slope):
    grid = cumulative_ranks(number_of, slope)
    lot = jax.random.randint(jax.random.fold_in(key, 1), dims, 0, int(grid[number_of - 1]))
    grade = jnp.searchsorted(jnp.asarray(grid, jnp.int32), lot, side="right")
    return jax.random.permutation(jax.random.fold_in(key, 2), number_of)[grade].astype(jnp.int32)


def length_profile(count, total, reach, skew):
    portions = [(1 << 20) // math.isqrt(standing ** skew) + 1 for standing in range(2, count + 1)]
    spare, counts = total - reach - (count - 1), [1] * (count - 1)
    while spare > 0:
        free = [i for i in range(count - 1) if counts[i] < reach]
        whole, budget = sum([portions[i] for i in free]), spare
        for i in free:
            more = min(reach - counts[i], max(1, budget * portions[i] // whole), spare)
            counts[i] = counts[i] + more
            spare = spare - more
    return np.array([reach] + counts)


def ragged(rng, amount, total, reach, slope):
    if amount == 2:
        one = jax.random.randint(rng, (), max(1, total - reach), min(reach, total - 1) + 1)
        return jnp.stack([one, total - one])
    lengths = jnp.asarray(length_profile(amount, total, reach, slope), jnp.int32)
    pairs = (amount - 1) // 2
    giver, sink = lengths[1:1 + 2 * pairs:2], lengths[2:2 + 2 * pairs:2]
    room = jnp.minimum(giver - 1, reach - sink)
    passed = jax.random.randint(jax.random.fold_in(rng, 1), (pairs,), 0, 1 << 20) % (room + 1)
    lengths = lengths.at[1:1 + 2 * pairs:2].set(giver - passed).at[2:2 + 2 * pairs:2].set(sink + passed)
    return lengths[jax.random.permutation(jax.random.fold_in(rng, 2), amount)]


def centred(stream_key, extent, width, bound, pieces=(), kind=jnp.bfloat16):
    values = jax.random.normal(stream_key, extent, jnp.float32) * width
    if len(pieces) > 0:
        values = shard_levels(stream_key, extent, pieces, -0.22, 0.18) * values
    return jnp.clip(values, min=-bound, max=bound).astype(kind)


def setup_inputs(seed: int = 0) -> dict:
    arg_keys = jax.random.split(jax.random.key(seed), 12)
    block_query = draw_block_query(jax.random.fold_in(arg_keys[11], 71), 0)
    block_key = draw_block_key(jax.random.fold_in(arg_keys[11], 71), 0)
    block_value = centred(arg_keys[2], (BLOCKS, WIDTH), 1.0, 6.0, ((0, 8), (1, 4)))
    block_doc = jnp.searchsorted(jnp.cumsum(ragged(arg_keys[3], DOCS, BLOCKS, BLOCKS - BLK_DEV, 0)), jnp.arange(BLOCKS), side="right").astype(jnp.int32)
    token_query = draw_token_query(jax.random.fold_in(arg_keys[11], 71), 0)
    token_key = draw_token_key(jax.random.fold_in(arg_keys[11], 71), 0)
    token_value = draw_token_value(jax.random.fold_in(arg_keys[11], 71), 0)
    token_state = centred(arg_keys[7], (TOKENS, WIDTH), 1.0, 6.0, ((0, 32),))
    norm_gain = jnp.clip(1.0 + 0.1 * jax.random.normal(arg_keys[8], (WIDTH,), jnp.float32), 0.5, 1.5)
    head_weight = draw_head_weight(jax.random.fold_in(arg_keys[11], 71), 0)
    targets = place_ends(ranked(arg_keys[10], (TOKENS,), VOCAB, 2), jax.random.fold_in(arg_keys[10], 3), 0, VOCAB - 1).astype(jnp.int32)
    return dict(block_query=block_query, block_key=block_key, block_value=block_value, block_doc=block_doc, token_query=token_query, token_key=token_key, token_value=token_value, token_state=token_state, norm_gain=norm_gain, head_weight=head_weight, targets=targets)


def global_mixing(block_query, block_key, block_value, block_doc):
    scale = 1.0 / math.sqrt(HEAD_DIM)
    queries = block_query.reshape(BLOCKS, HEADS, HEAD_DIM).astype(jnp.float32)
    keys = block_key.reshape(BLOCKS, HEADS, HEAD_DIM).astype(jnp.float32)
    values = block_value.reshape(BLOCKS, HEADS, HEAD_DIM).astype(jnp.float32)
    scores = jnp.einsum('qhd,khd->qhk', queries, keys) * scale
    places = jnp.arange(BLOCKS, dtype=jnp.int32)
    allowed = (places[:, None] >= places[None, :]) & (block_doc[:, None] == block_doc[None, :])
    scores = jnp.where(allowed[:, None, :], scores, -jnp.inf)
    highest = lax.optimization_barrier(jnp.max(scores, axis=-1, keepdims=True))
    weights = jnp.exp(scores - highest)
    totals = lax.optimization_barrier(jnp.sum(weights, axis=-1))
    rounded = lax.optimization_barrier(weights.astype(jnp.bfloat16)).astype(jnp.float32)
    mixed = jnp.einsum('qhk,khd->qhd', rounded, values) / totals[:, :, None]
    return mixed.reshape(BLOCKS, WIDTH).astype(jnp.bfloat16)

def local_decoder(context, token_query, token_key, token_value, token_state, norm_gain):
    scale = 1.0 / math.sqrt(HEAD_DIM)
    groups = context.shape[0]
    shape = (groups, BLOCK_LEN, HEADS, HEAD_DIM)
    prefix = context.reshape(groups, 1, HEADS, HEAD_DIM)
    queries = token_query.reshape(shape).astype(jnp.float32)
    keys = jnp.concatenate([prefix, token_key.reshape(shape)], axis=1).astype(jnp.float32)
    values = jnp.concatenate([prefix, token_value.reshape(shape)], axis=1).astype(jnp.float32)
    scores = jnp.einsum('bihd,bjhd->bhij', queries, keys) * scale
    allowed = jnp.arange(BLOCK_LEN + 1, dtype=jnp.int32)[None, :] <= jnp.arange(BLOCK_LEN, dtype=jnp.int32)[:, None] + 1
    scores = jnp.where(allowed, scores, -jnp.inf)
    highest = lax.optimization_barrier(jnp.max(scores, axis=-1, keepdims=True))
    weights = jnp.exp(scores - highest)
    totals = lax.optimization_barrier(jnp.sum(weights, axis=-1))
    rounded = lax.optimization_barrier(weights.astype(jnp.bfloat16)).astype(jnp.float32)
    mixed = jnp.einsum('bhij,bjhd->bihd', rounded, values) / jnp.transpose(totals, (0, 2, 1))[..., None]
    summed = token_state.astype(jnp.float32) + mixed.reshape(groups * BLOCK_LEN, WIDTH)
    power = lax.optimization_barrier(jnp.mean(summed * summed, axis=-1, keepdims=True))
    return (summed * lax.rsqrt(power + 1e-05) * norm_gain).astype(jnp.bfloat16)

def token_priors(hidden, head_weight, targets):
    span = math.gcd(TOKENS, 256)

    def one_block(pair):
        rows, wanted = pair
        logits = jnp.dot(rows, head_weight, preferred_element_type=jnp.float32)
        highest = lax.optimization_barrier(jnp.max(logits, axis=-1))
        totals = lax.optimization_barrier(jnp.sum(jnp.exp(logits - highest[:, None]), axis=-1))
        picked = jnp.take_along_axis(logits, wanted[:, None].astype(jnp.int32), axis=1)[:, 0]
        return picked - (highest + jnp.log(totals))
    result = lax.map(one_block, (hidden.reshape(TOKENS // span, span, WIDTH), targets.reshape(TOKENS // span, span)))
    return result.reshape(TOKENS)

def reference(block_query, block_key, block_value, block_doc, token_query, token_key, token_value, token_state, norm_gain, head_weight, targets):
    block_context = global_mixing(block_query, block_key, block_value, block_doc)
    hidden = local_decoder(block_context, token_query, token_key, token_value, token_state, norm_gain)
    return (block_context, token_priors(hidden, head_weight, targets))
```

```python
import functools
import math

import jax
import jax.numpy as jnp
from jax import lax
from jax.experimental import pallas as pl
from jax.experimental.pallas import tpu as pltpu
from jax.sharding import PartitionSpec as P

HEAD_DIM = 128
BLOCK_LEN = 4
MESH = pl.DeviceIdType.MESH

big_negative = -1e30


def local_decoder(context, token_query, token_key, token_value, token_state, norm_gain):
    scale = 1.0 / math.sqrt(HEAD_DIM)
    groups = context.shape[0]
    width = context.shape[1]
    head_total = width // HEAD_DIM
    shape = (groups, BLOCK_LEN, head_total, HEAD_DIM)
    prefix = context.reshape(groups, 1, head_total, HEAD_DIM)
    queries = token_query.reshape(shape)
    keys = jnp.concatenate([prefix, token_key.reshape(shape)], axis=1)
    values = jnp.concatenate([prefix, token_value.reshape(shape)], axis=1)
    scores = (
        jnp.einsum("bihd,bjhd->bhij", queries, keys, preferred_element_type=jnp.float32) * scale
    )
    allowed = (
        jnp.arange(BLOCK_LEN + 1, dtype=jnp.int32)[None, :]
        <= jnp.arange(BLOCK_LEN, dtype=jnp.int32)[:, None] + 1
    )
    scores = jnp.where(allowed, scores, -jnp.inf)
    highest = jnp.max(scores, axis=-1, keepdims=True)
    weights = jnp.exp(scores - highest)
    totals = jnp.sum(weights, axis=-1)
    mixed = jnp.einsum(
        "bhij,bjhd->bihd", weights.astype(jnp.bfloat16), values, preferred_element_type=jnp.float32
    )
    mixed = mixed / jnp.transpose(totals, (0, 2, 1))[..., None]
    summed = token_state.astype(jnp.float32) + mixed.reshape(groups * BLOCK_LEN, width)
    power = jnp.mean(summed * summed, axis=-1, keepdims=True)
    return (summed * lax.rsqrt(power + 1e-05) * norm_gain).astype(jnp.bfloat16)


class Place:
    def __init__(self, ctx_size, vocab_size):
        self.nv = vocab_size
        self.chips = ctx_size // 2
        self.bits = [1 << i for i in range(self.chips.bit_length() - 1)]
        assert ctx_size == 2 << len(self.bits) and vocab_size % 2 == 0
        self.ctx = lax.axis_index("ctx")
        self.z = lax.axis_index("vocab")

    def flip(self, mask):
        ctx, out, bit = self.ctx, self.ctx, 1
        while bit <= mask:
            if mask & bit:
                has = lax.rem(lax.div(ctx, bit), 2)
                out = out + bit - 2 * bit * has
            bit *= 2
        return out

    def device(self, r, s, c):
        return (self.flip(2 * r + c), lax.rem(self.z + (self.nv - s) % self.nv, self.nv))

    def slot(self, r, s, c):
        return (r * self.nv + s) * 2 + c

    def onward(self, r, half):
        if r == 0:
            return list(self.bits)
        if half == 0:
            return [b for b in self.bits if b > r]
        return [b for b in self.bits if b < (r & -r)]


def entry_barrier(place):
    barrier = pltpu.get_barrier_semaphore()
    count = 0
    for r in range(place.chips):
        for s in range(place.nv):
            for c in range(2):
                if r or s or c:
                    pl.semaphore_signal(
                        barrier, inc=1, device_id=place.device(r, s, c), device_id_type=MESH
                    )
                    count += 1
    pl.semaphore_wait(barrier, count)


def head_kernel(
    sizes, h_ref, w_hbm, t_ref, o_ref, rows, w_ref, logits, t_col, s_out, s_in,
    w_sem, send, recv, s_send, s_recv,
):
    place = Place(*sizes)
    nv, chips = place.nv, place.chips
    tok, width = h_ref.shape
    cols = w_ref.shape[1]
    half_width = width // 2
    per_group = nv * 2
    group = per_group * tok
    load_w = pltpu.make_async_copy(w_hbm, w_ref, w_sem)
    load_w.start()
    rows[pl.ds(0, tok), :] = h_ref[...]
    entry_barrier(place)

    sent = []

    def view(slot, half):
        return rows.at[pl.ds(slot * tok, tok), pl.ds(half * half_width, half_width)]

    def push(src, half, dst, device):
        dst_slot = place.slot(*dst)
        copy = pltpu.make_async_remote_copy(
            src_ref=view(place.slot(*src), half),
            dst_ref=view(dst_slot, half),
            send_sem=send.at[len(sent)],
            recv_sem=recv.at[2 * dst_slot + half],
            device_id=device,
            device_id_type=MESH,
        )
        copy.start()
        sent.append(copy)

    def arrived(r, s, c, half):
        slot = place.slot(r, s, c)
        pltpu.make_async_copy(view(slot, half), view(slot, half), recv.at[2 * slot + half]).wait()

    def along_vocab(s, half):
        mid = nv // 2
        ahead = s < mid - 1 or (s == mid - 1 and half == 0)
        back = s == 0 or s > mid + 1 or (s == mid + 1 and half == 1)
        if s == 0:
            ahead = mid > 1 or half == 0
            back = mid > 1 or half == 1
        if ahead:
            push((0, s, 0), half, (0, s + 1, 0), place.device(0, nv - 1, 0))
        if back:
            push((0, s, 0), half, (0, (s - 1) % nv, 0), place.device(0, 1, 0))

    def pass_on(r, s, half):
        if r == 0:
            along_vocab(s, half)
        for bit in place.onward(r, half):
            push((r, s, 0), half, (r ^ bit, s, 0), place.device(bit, 0, 0))
        push((r, s, 0), half, (r, s, 1), place.device(0, 0, 1))

    order = [0]
    for d in range(1, nv // 2):
        order += [d, nv - d]
    order.append(nv // 2)

    def take(r, s):
        for half in range(2):
            if r or s:
                arrived(r, s, 0, half)
            pass_on(r, s, half)

    for half in range(2):
        along_vocab(0, half)
    for half in range(2):
        for bit in place.bits:
            push((0, 0, 0), half, (bit, 0, 0), place.device(bit, 0, 0))
    for half in range(2):
        push((0, 0, 0), half, (0, 0, 1), place.device(0, 0, 1))

    first = place.ctx * nv + place.z

    def place_targets(r):
        for s in range(nv):
            for c in range(2):
                ctx, z = place.device(r, s, c)
                start = pl.multiple_of((ctx * nv + z) * tok, tok)
                t_col[pl.ds(place.slot(r, s, c) * tok, tok), :] = t_ref[pl.ds(start, tok), :]

    for r in range(chips):
        place_targets(r)

    s_sent = []
    lane = lax.broadcasted_iota(jnp.int32, (tok, 128), 1)
    column = lax.broadcasted_iota(jnp.int32, (tok, cols), 1) + first * cols
    tile = min(256, cols)

    def compute(r):
        for s in range(nv):
            for half in range(2):
                arrived(r, s, 1, half)
        base = r * group

        @pl.loop(0, cols // tile)
        def _(n):
            at = pl.ds(pl.multiple_of(n * tile, tile), tile)
            logits[:, at] = jnp.dot(
                rows[pl.ds(base, group), :], w_ref[:, at], preferred_element_type=jnp.float32
            )

        @pl.loop(0, per_group)
        def _(i):
            at = pl.multiple_of(i * tok, tok)
            block = logits[pl.ds(at, tok), :]
            top = jnp.max(block, axis=1, keepdims=True)
            mass = jnp.sum(jnp.exp(block - top), axis=1, keepdims=True)
            wanted = t_col[pl.ds(pl.multiple_of(base + at, tok), tok), :]
            pick = jnp.sum(jnp.where(column == wanted, block, 0.0), axis=1, keepdims=True)
            packed = jnp.where(lane == 0, top, jnp.where(lane == 1, mass, pick))
            if tok < 128:
                packed = jnp.concatenate(
                    [packed, jnp.zeros((128 - tok, 128), jnp.float32)], axis=0
                )
            s_out[r * per_group + i] = jnp.transpose(packed)[0:8, :]

        for s in range(nv):
            for c in range(2):
                slot, there = place.slot(r, s, c), place.slot(r, (nv - s) % nv, c)
                if r or s or c:
                    copy = pltpu.make_async_remote_copy(
                        src_ref=s_out.at[slot],
                        dst_ref=s_in.at[there],
                        send_sem=s_send.at[slot],
                        recv_sem=s_recv.at[there],
                        device_id=place.device(r, s, c),
                        device_id_type=MESH,
                    )
                    copy.start()
                    s_sent.append(copy)
                else:
                    s_in[0] = s_out[0]

    outer = list(range(1, chips))
    outer.sort(key=lambda r: (bin(r).count("1"), r))
    near = [r for r in outer if r in place.bits]
    far = [r for r in outer if r not in place.bits]
    for r in near:
        take(r, 0)
    for s in order[1:]:
        take(0, s)
    for r in far:
        take(r, 0)
    for r in near:
        for s in order[1:-1]:
            take(r, s)
    load_w.wait()
    compute(0)
    for r in near:
        take(r, order[-1])
    for r in far:
        for s in order[1:-1]:
            take(r, s)
    for r in near:
        compute(r)
    for r in far:
        take(r, order[-1])
    for r in far:
        compute(r)

    for copy in s_sent:
        copy.wait_recv()
    stats = s_in[...]
    tops = stats[:, 0:1, :]
    top = jnp.max(tops, axis=0)
    mass = jnp.sum(stats[:, 1:2, :] * jnp.exp(tops - top[None]), axis=0)
    pick = jnp.sum(stats[:, 2:3, :], axis=0)
    prior = pick - (top + jnp.log(mass))
    o_ref[...] = prior
    for copy in s_sent:
        copy.wait_send()
    for copy in sent:
        copy.wait_send()


def head_priors(sizes, hidden, head_weight, targets):
    ctx_size, nv = sizes
    tok, width = hidden.shape
    cols = head_weight.shape[1]
    devices = ctx_size * nv
    tokens = devices * tok
    out = pl.pallas_call(
        functools.partial(head_kernel, sizes),
        out_shape=jax.ShapeDtypeStruct((1, 128), jnp.float32),
        in_specs=[
            pl.BlockSpec(memory_space=pltpu.VMEM),
            pl.BlockSpec(memory_space=pl.ANY),
            pl.BlockSpec(memory_space=pltpu.VMEM),
        ],
        out_specs=pl.BlockSpec(memory_space=pltpu.VMEM),
        scratch_shapes=[
            pltpu.VMEM((tokens, width), jnp.bfloat16),
            pltpu.VMEM((width, cols), jnp.bfloat16),
            pltpu.VMEM((nv * 2 * tok, cols), jnp.float32),
            pltpu.VMEM((tokens, 1), jnp.int32),
            pltpu.VMEM((devices, 8, 128), jnp.float32),
            pltpu.VMEM((devices, 8, 128), jnp.float32),
            pltpu.SemaphoreType.DMA,
            pltpu.SemaphoreType.DMA((2 * devices,)),
            pltpu.SemaphoreType.DMA((2 * devices,)),
            pltpu.SemaphoreType.DMA((devices,)),
            pltpu.SemaphoreType.DMA((devices,)),
        ],
        compiler_params=pltpu.CompilerParams(
            collective_id=0, has_side_effects=True, vmem_limit_bytes=58 * 1024 * 1024
        ),
        name="head_priors",
    )(hidden, head_weight, targets.reshape(tokens, 1))
    return out[0, :tok]


def local(
    sizes,
    block_query,
    block_key,
    block_value,
    block_doc,
    token_query,
    token_key,
    token_value,
    token_state,
    norm_gain,
    head_weight,
    targets,
):
    local_rows = block_query.shape[0]
    head_count = block_query.shape[1] // HEAD_DIM
    scale = 1.0 / math.sqrt(HEAD_DIM)
    first_row = lax.axis_index("ctx") * local_rows
    queries = block_query.reshape(local_rows, head_count, HEAD_DIM)
    own_doc = block_doc.astype(jnp.bfloat16)
    query_places = first_row + jnp.arange(local_rows, dtype=jnp.int32)
    keys = lax.all_gather(block_key, "ctx", axis=0, tiled=True)
    values = lax.all_gather(block_value, "ctx", axis=0, tiled=True)
    docs = lax.all_gather(own_doc, "ctx", axis=0, tiled=True)
    count = keys.shape[0]
    keys = keys.reshape(count, head_count, HEAD_DIM)
    values = values.reshape(count, head_count, HEAD_DIM)
    scores = jnp.einsum("qhd,khd->qhk", queries, keys, preferred_element_type=jnp.float32) * scale
    key_places = jnp.arange(count, dtype=jnp.int32)
    allowed = (query_places[:, None] >= key_places[None, :]) & (own_doc[:, None] == docs[None, :])
    allowed = allowed[:, None, :]
    newest = jnp.max(jnp.where(allowed, scores, big_negative), axis=-1)
    weights = jnp.where(allowed, jnp.exp(scores - newest[..., None]), 0.0)
    totals = jnp.sum(weights, axis=-1)
    mixed = jnp.einsum(
        "qhk,khd->qhd", weights.astype(jnp.bfloat16), values, preferred_element_type=jnp.float32
    )
    block_context = (
        (mixed / totals[..., None]).reshape(local_rows, head_count * HEAD_DIM).astype(jnp.bfloat16)
    )
    grouped = lax.all_to_all(block_context, "vocab", split_axis=0, concat_axis=1, tiled=True)
    hidden = local_decoder(grouped, token_query, token_key, token_value, token_state, norm_gain)
    return (block_context, head_priors(sizes, hidden, head_weight, targets))


def solution(mesh):
    placed = (
        P("ctx", "vocab"),
        P("ctx", "vocab"),
        P("ctx", "vocab"),
        P("ctx"),
        P(("ctx", "vocab"), None),
        P(("ctx", "vocab"), None),
        P(("ctx", "vocab"), None),
        P(("ctx", "vocab"), None),
        P(),
        P(None, ("ctx", "vocab")),
        P(),
    )
    return jax.shard_map(
        functools.partial(local, (mesh.shape["ctx"], mesh.shape["vocab"])),
        mesh=mesh,
        in_specs=placed,
        out_specs=(P("ctx", "vocab"), P(("ctx", "vocab"))),
        check_vma=False,
    )
```

```python
import functools
import math

import jax
import jax.numpy as jnp
from jax import lax
from jax.experimental import pallas as pl
from jax.experimental.pallas import tpu as pltpu
from jax.sharding import PartitionSpec as P

HEAD_DIM = 128
BLOCK_LEN = 4
MESH = pl.DeviceIdType.MESH

big_negative = -1e30


class Place:
    def __init__(self, ctx_size, vocab_size):
        self.nv = vocab_size
        self.chips = ctx_size // 2
        self.bits = [1 << i for i in range(self.chips.bit_length() - 1)]
        assert ctx_size == 2 << len(self.bits) and vocab_size % 2 == 0
        self.ctx = lax.axis_index("ctx")
        self.z = lax.axis_index("vocab")

    def flip(self, mask):
        ctx, out, bit = self.ctx, self.ctx, 1
        while bit <= mask:
            if mask & bit:
                has = lax.rem(lax.div(ctx, bit), 2)
                out = out + bit - 2 * bit * has
            bit *= 2
        return out

    def device(self, r, s, c):
        return (self.flip(2 * r + c), lax.rem(self.z + (self.nv - s) % self.nv, self.nv))

    def slot(self, r, s, c):
        return (r * self.nv + s) * 2 + c

    def onward(self, r, half):
        if r == 0:
            return list(self.bits)
        if half == 0:
            return [b for b in self.bits if b > r]
        return [b for b in self.bits if b < (r & -r)]


def entry_barrier(place):
    barrier = pltpu.get_barrier_semaphore()
    count = 0
    for r in range(place.chips):
        for s in range(place.nv):
            for c in range(2):
                if r or s or c:
                    pl.semaphore_signal(
                        barrier, inc=1, device_id=place.device(r, s, c), device_id_type=MESH
                    )
                    count += 1
    pl.semaphore_wait(barrier, count)


def up_to(value, unit):
    return (value + unit - 1) // unit * unit


def kernel(
    sizes, bq_hbm, bk_hbm, bv_hbm, doc_ref, tq_hbm, tk_hbm, tv_hbm, ts_hbm, g_ref, w_hbm, t_ref,
    bc_ref, o_ref,
    bq, kv, doc_in, c_all, c_out, c_in, tq, kcat, vcat, ts, summed,
    rows, w_ref, logits, t_col, s_out, s_in,
    in_sems, kv_send, kv_recv, d_send, d_recv, c_send, c_recv,
    w_sem, send, recv, s_send, s_recv,
):
    place = Place(*sizes)
    nv, chips = place.nv, place.chips
    tok, width = ts.shape
    cols = w_ref.shape[1]
    half_width = width // 2
    per_group = nv * 2
    group = per_group * tok
    blk, part = bq.shape
    scale = 1.0 / math.sqrt(HEAD_DIM)
    heads = part // HEAD_DIM
    share = blk // nv
    pad8, pad16 = up_to(share, 8), up_to(share, 16)

    loads = [
        pltpu.make_async_copy(bk_hbm, kv.at[0, pl.ds(0, blk)], in_sems.at[0]),
        pltpu.make_async_copy(bv_hbm, kv.at[1, pl.ds(0, blk)], in_sems.at[1]),
        pltpu.make_async_copy(bq_hbm, bq, in_sems.at[2]),
        pltpu.make_async_copy(tq_hbm, tq, in_sems.at[3]),
        pltpu.make_async_copy(tk_hbm, kcat.at[pl.ds(0, tok)], in_sems.at[4]),
        pltpu.make_async_copy(tv_hbm, vcat.at[pl.ds(0, tok)], in_sems.at[5]),
        pltpu.make_async_copy(ts_hbm, ts, in_sems.at[6]),
    ]
    for load in loads:
        load.start()
    load_w = pltpu.make_async_copy(w_hbm, w_ref, w_sem)
    load_w.start()

    lane8 = lax.broadcasted_iota(jnp.int32, (8, 128), 1)
    doc_in[0] = jnp.zeros((8, 128), jnp.float32)
    doc_in[0, 0:1, 0:blk] = doc_ref[...].astype(jnp.float32)
    tiled = doc_in[0]
    span = blk
    while span < 128:
        tiled = tiled + pltpu.roll(tiled, span, 1)
        span *= 2
    doc_in[0] = tiled
    entry_barrier(place)

    kv_sent = []

    def kv_view(r, c, half):
        return kv.at[half, pl.ds((2 * r + c) * blk, blk)]

    def kv_push(src, half, dst, device):
        copy = pltpu.make_async_remote_copy(
            src_ref=kv_view(*src, half),
            dst_ref=kv_view(*dst, half),
            send_sem=kv_send.at[len(kv_sent)],
            recv_sem=kv_recv.at[2 * (2 * dst[0] + dst[1]) + half],
            device_id=device,
            device_id_type=MESH,
        )
        copy.start()
        kv_sent.append(copy)

    def kv_arrived(r, c, half):
        ref = kv_view(r, c, half)
        pltpu.make_async_copy(ref, ref, kv_recv.at[2 * (2 * r + c) + half]).wait()

    def kv_pass(r, half):
        for bit in place.onward(r, half):
            kv_push((r, 0), half, (r ^ bit, 0), place.device(bit, 0, 0))
        kv_push((r, 0), half, (r, 1), place.device(0, 0, 1))

    nearest = sorted(range(1, chips), key=lambda r: (bin(r).count("1"), r))
    for half in range(2):
        loads[half].wait()
        kv_pass(0, half)
    d_sent = []
    for r in range(chips):
        for c in range(2):
            slot = 2 * r + c
            if slot:
                copy = pltpu.make_async_remote_copy(
                    src_ref=doc_in.at[0],
                    dst_ref=doc_in.at[slot],
                    send_sem=d_send.at[slot],
                    recv_sem=d_recv.at[slot],
                    device_id=place.device(r, 0, c),
                    device_id_type=MESH,
                )
                copy.start()
                d_sent.append(copy)

    t_lane = lax.broadcasted_iota(jnp.int32, (tok, 128), 1)
    t_row = lax.broadcasted_iota(jnp.int32, (tok, 128), 0)
    in_row = 128 // tok
    for r in range(chips):
        for s in range(nv):
            for c in range(2):
                ctx, z = place.device(r, s, c)
                flat = ctx * nv + z
                line = t_ref[pl.ds(lax.div(flat, in_row), 1), :].astype(jnp.float32)
                here = t_lane == t_row + lax.rem(flat, in_row) * tok
                t_col[pl.ds(place.slot(r, s, c) * tok, tok), :] = jnp.sum(
                    jnp.where(here, line, 0.0), axis=1, keepdims=True
                )

    for r in nearest:
        for half in range(2):
            kv_arrived(r, 0, half)
            kv_pass(r, half)

    q_lane = lax.broadcasted_iota(jnp.int32, (blk, 128), 1)
    q_row = lax.broadcasted_iota(jnp.int32, (blk, 128), 0)
    own_doc = jnp.sum(jnp.where(q_lane == q_row, tiled[0:1, :], 0.0), axis=1, keepdims=True)
    own_place = q_row + place.ctx * blk
    for copy in d_sent:
        copy.wait_recv()
    masks = []
    fit = 128 // blk
    for first in range(0, 2 * chips, fit):
        docs = jnp.zeros((1, 128), jnp.float32)
        places = jnp.zeros((blk, 128), jnp.int32)
        for k in range(fit):
            slot = first + k
            mine = (q_lane >= k * blk) & (q_lane < (k + 1) * blk)
            docs = jnp.where(mine[0:1, :], doc_in[slot, 0:1, :], docs)
            places = jnp.where(mine, place.flip(slot) * blk - k * blk + q_lane, places)
        masks.append(((own_doc == docs) & (own_place >= places)).astype(jnp.float32))
    allowed = (jnp.concatenate(masks, axis=1) > 0.5)[None]
    loads[2].wait()
    for r in range(chips):
        for half in range(2):
            kv_arrived(r, 1, half)

    def softmax(scores, allowed):
        scores = jnp.where(allowed, scores * scale, big_negative)
        top = jnp.max(scores, axis=-1, keepdims=True)
        weights = jnp.where(allowed, jnp.exp(scores - top), 0.0)
        return weights.astype(jnp.bfloat16), jnp.sum(weights, axis=-1, keepdims=True)

    def dot_t(a, b):
        return lax.dot_general(a, b, (((1,), (1,)), ((), ())), preferred_element_type=jnp.float32)

    ats = [pl.ds(h * HEAD_DIM, HEAD_DIM) for h in range(heads)]
    scores = jnp.stack([dot_t(bq[:, at], kv[0, :, at]) for at in ats])
    weights, totals = softmax(scores, allowed)
    if pad8 > share:
        c_out[...] = jnp.zeros_like(c_out)
    for h, at in enumerate(ats):
        mixed = jnp.dot(weights[h], kv[1, :, at], preferred_element_type=jnp.float32) / totals[h]
        rounded = mixed.astype(jnp.bfloat16)
        bc_ref[:, at] = rounded
        c_all[:, at] = rounded.astype(jnp.float32)
    for v in range(nv):
        c_out[v, 0:share, :] = c_all[v * share:(v + 1) * share, :]

    c_sent = []
    for s in sorted(range(1, nv), key=lambda s: -min(s, nv - s)):
        device = place.device(0, s, 0)
        copy = pltpu.make_async_remote_copy(
            src_ref=c_out.at[device[1]],
            dst_ref=c_in.at[place.z],
            send_sem=c_send.at[s],
            recv_sem=c_recv.at[s],
            device_id=device,
            device_id_type=MESH,
        )
        copy.start()
        c_sent.append(copy)
    c_in[place.z] = c_out[place.z]

    deep = tok + pad16
    l_row = lax.broadcasted_iota(jnp.int32, (tok, deep), 0)
    l_col = lax.broadcasted_iota(jnp.int32, (tok, deep), 1)
    l_block = lax.div(l_row, BLOCK_LEN)
    usable = (l_col < tok) & (l_col <= l_row) & (lax.div(l_col, BLOCK_LEN) == l_block)
    usable = (usable | (l_col == tok + l_block))[None]
    for load in loads[3:]:
        load.wait()
    for copy in c_sent:
        copy.wait_recv()

    def decode(v, power):
        context = c_in[v]
        if pad16 > pad8:
            context = jnp.concatenate(
                [context, jnp.zeros((pad16 - pad8, part), jnp.float32)], axis=0
            )
        context = context.astype(jnp.bfloat16)
        start = pl.multiple_of(v * part, part)
        kcat[pl.ds(tok, pad16), pl.ds(start, part)] = context
        vcat[pl.ds(tok, pad16), pl.ds(start, part)] = context
        spots = [pl.ds(pl.multiple_of(start + h * HEAD_DIM, HEAD_DIM), HEAD_DIM) for h in range(heads)]
        scores = jnp.stack([dot_t(tq[:, at], kcat[:, at]) for at in spots])
        weights, totals = softmax(scores, usable)
        for h, at in enumerate(spots):
            mixed = jnp.dot(weights[h], vcat[:, at], preferred_element_type=jnp.float32)
            total = ts[:, at].astype(jnp.float32) + mixed / totals[h]
            summed[:, at] = total
            power = power + total * total
        return power

    power = lax.fori_loop(0, nv, decode, jnp.zeros((tok, HEAD_DIM), jnp.float32))
    power = jnp.sum(power, axis=1, keepdims=True) / width
    rows[pl.ds(0, tok), :] = (
        summed[...] * lax.rsqrt(power + 1e-05) * g_ref[...]
    ).astype(jnp.bfloat16)

    sent = []

    def view(slot, half):
        return rows.at[pl.ds(slot * tok, tok), pl.ds(half * half_width, half_width)]

    def push(src, half, dst, device):
        dst_slot = place.slot(*dst)
        copy = pltpu.make_async_remote_copy(
            src_ref=view(place.slot(*src), half),
            dst_ref=view(dst_slot, half),
            send_sem=send.at[len(sent)],
            recv_sem=recv.at[2 * dst_slot + half],
            device_id=device,
            device_id_type=MESH,
        )
        copy.start()
        sent.append(copy)

    def arrived(r, s, c, half):
        slot = place.slot(r, s, c)
        pltpu.make_async_copy(view(slot, half), view(slot, half), recv.at[2 * slot + half]).wait()

    def along_vocab(s, half):
        mid = nv // 2
        ahead = s < mid - 1 or (s == mid - 1 and half == 0)
        back = s == 0 or s > mid + 1 or (s == mid + 1 and half == 1)
        if s == 0:
            ahead = mid > 1 or half == 0
            back = mid > 1 or half == 1
        if ahead:
            push((0, s, 0), half, (0, s + 1, 0), place.device(0, nv - 1, 0))
        if back:
            push((0, s, 0), half, (0, (s - 1) % nv, 0), place.device(0, 1, 0))

    def pass_on(r, s, half):
        if r == 0:
            along_vocab(s, half)
        for bit in place.onward(r, half):
            push((r, s, 0), half, (r ^ bit, s, 0), place.device(bit, 0, 0))
        push((r, s, 0), half, (r, s, 1), place.device(0, 0, 1))

    order = [0]
    for d in range(1, nv // 2):
        order += [d, nv - d]
    order.append(nv // 2)

    def take(r, s):
        for half in range(2):
            if r or s:
                arrived(r, s, 0, half)
            pass_on(r, s, half)

    for half in range(2):
        along_vocab(0, half)
    for half in range(2):
        for bit in place.bits:
            push((0, 0, 0), half, (bit, 0, 0), place.device(bit, 0, 0))
    for half in range(2):
        push((0, 0, 0), half, (0, 0, 1), place.device(0, 0, 1))

    first = place.ctx * nv + place.z
    s_sent = []
    lane = lax.broadcasted_iota(jnp.int32, (tok, 128), 1)
    column = lax.broadcasted_iota(jnp.int32, (tok, cols), 1) + first * cols
    column = column.astype(jnp.float32)
    tile = min(256, cols)

    def compute(r):
        for s in range(nv):
            for half in range(2):
                arrived(r, s, 1, half)
        base = r * group

        @pl.loop(0, cols // tile)
        def _(n):
            at = pl.ds(pl.multiple_of(n * tile, tile), tile)
            logits[:, at] = jnp.dot(
                rows[pl.ds(base, group), :], w_ref[:, at], preferred_element_type=jnp.float32
            )

        @pl.loop(0, per_group)
        def _(i):
            at = pl.multiple_of(i * tok, tok)
            block = logits[pl.ds(at, tok), :]
            top = jnp.max(block, axis=1, keepdims=True)
            mass = jnp.sum(jnp.exp(block - top), axis=1, keepdims=True)
            wanted = t_col[pl.ds(pl.multiple_of(base + at, tok), tok), :]
            pick = jnp.sum(jnp.where(column == wanted, block, 0.0), axis=1, keepdims=True)
            packed = jnp.where(lane == 0, top, jnp.where(lane == 1, mass, pick))
            if tok < 128:
                packed = jnp.concatenate(
                    [packed, jnp.zeros((128 - tok, 128), jnp.float32)], axis=0
                )
            s_out[r * per_group + i] = jnp.transpose(packed)[0:8, :]

        for s in range(nv):
            for c in range(2):
                slot, there = place.slot(r, s, c), place.slot(r, (nv - s) % nv, c)
                if r or s or c:
                    copy = pltpu.make_async_remote_copy(
                        src_ref=s_out.at[slot],
                        dst_ref=s_in.at[there],
                        send_sem=s_send.at[slot],
                        recv_sem=s_recv.at[there],
                        device_id=place.device(r, s, c),
                        device_id_type=MESH,
                    )
                    copy.start()
                    s_sent.append(copy)
                else:
                    s_in[0] = s_out[0]

    outer = list(range(1, chips))
    outer.sort(key=lambda r: (bin(r).count("1"), r))
    near = [r for r in outer if r in place.bits]
    far = [r for r in outer if r not in place.bits]
    for r in near:
        take(r, 0)
    for s in order[1:]:
        take(0, s)
    for r in far:
        take(r, 0)
    for r in near:
        for s in order[1:-1]:
            take(r, s)
    load_w.wait()
    compute(0)
    for r in near:
        take(r, order[-1])
    for r in far:
        for s in order[1:-1]:
            take(r, s)
    for r in near:
        compute(r)
    for r in far:
        take(r, order[-1])
    for r in far:
        compute(r)

    for copy in s_sent:
        copy.wait_recv()
    stats = s_in[...]
    tops = stats[:, 0:1, :]
    top = jnp.max(tops, axis=0)
    mass = jnp.sum(stats[:, 1:2, :] * jnp.exp(tops - top[None]), axis=0)
    pick = jnp.sum(stats[:, 2:3, :], axis=0)
    prior = pick - (top + jnp.log(mass))
    o_ref[...] = prior[:, 0:tok]
    for copy in s_sent:
        copy.wait_send()
    for copy in sent + kv_sent + d_sent + c_sent:
        copy.wait_send()


def local(
    sizes,
    block_query,
    block_key,
    block_value,
    block_doc,
    token_query,
    token_key,
    token_value,
    token_state,
    norm_gain,
    head_weight,
    targets,
):
    ctx_size, nv = sizes
    blk, part = block_query.shape
    tok, width = token_state.shape
    cols = head_weight.shape[1]
    devices = ctx_size * nv
    tokens = devices * tok
    share = blk // nv
    pad8, pad16 = up_to(share, 8), up_to(share, 16)
    vmem = pl.BlockSpec(memory_space=pltpu.VMEM)
    hbm = pl.BlockSpec(memory_space=pl.ANY)
    dma = pltpu.SemaphoreType.DMA
    bf16, f32 = jnp.bfloat16, jnp.float32
    context, prior = pl.pallas_call(
        functools.partial(kernel, sizes),
        out_shape=(
            jax.ShapeDtypeStruct((blk, part), bf16),
            jax.ShapeDtypeStruct((1, tok), f32),
        ),
        in_specs=[hbm, hbm, hbm, vmem, hbm, hbm, hbm, hbm, vmem, hbm, vmem],
        out_specs=(vmem, vmem),
        scratch_shapes=[
            pltpu.VMEM((blk, part), bf16),
            pltpu.VMEM((2, ctx_size * blk, part), bf16),
            pltpu.VMEM((ctx_size, 8, 128), f32),
            pltpu.VMEM((blk, part), f32),
            pltpu.VMEM((nv, pad8, part), f32),
            pltpu.VMEM((nv, pad8, part), f32),
            pltpu.VMEM((tok, width), bf16),
            pltpu.VMEM((tok + pad16, width), bf16),
            pltpu.VMEM((tok + pad16, width), bf16),
            pltpu.VMEM((tok, width), bf16),
            pltpu.VMEM((tok, width), f32),
            pltpu.VMEM((tokens, width), bf16),
            pltpu.VMEM((width, cols), bf16),
            pltpu.VMEM((nv * 2 * tok, cols), f32),
            pltpu.VMEM((tokens, 1), f32),
            pltpu.VMEM((devices, 8, 128), f32),
            pltpu.VMEM((devices, 8, 128), f32),
            dma((7,)),
            dma((2 * ctx_size,)),
            dma((2 * ctx_size,)),
            dma((ctx_size,)),
            dma((ctx_size,)),
            dma((nv,)),
            dma((nv,)),
            dma,
            dma((2 * devices,)),
            dma((2 * devices,)),
            dma((devices,)),
            dma((devices,)),
        ],
        compiler_params=pltpu.CompilerParams(
            collective_id=0, has_side_effects=True, vmem_limit_bytes=60 * 1024 * 1024
        ),
        name="window",
    )(
        block_query,
        block_key,
        block_value,
        block_doc.reshape(1, blk),
        token_query,
        token_key,
        token_value,
        token_state,
        norm_gain.reshape(1, width),
        head_weight,
        targets.reshape(tokens // 128, 128),
    )
    return context, prior.reshape(tok)


def solution(mesh):
    placed = (
        P("ctx", "vocab"),
        P("ctx", "vocab"),
        P("ctx", "vocab"),
        P("ctx"),
        P(("ctx", "vocab"), None),
        P(("ctx", "vocab"), None),
        P(("ctx", "vocab"), None),
        P(("ctx", "vocab"), None),
        P(),
        P(None, ("ctx", "vocab")),
        P(),
    )
    return jax.shard_map(
        functools.partial(local, (mesh.shape["ctx"], mesh.shape["vocab"])),
        mesh=mesh,
        in_specs=placed,
        out_specs=(P("ctx", "vocab"), P(("ctx", "vocab"))),
        check_vma=False,
    )
```

```python
import functools
import math

import jax
import jax.numpy as jnp
from jax import lax
from jax.experimental import pallas as pl
from jax.experimental.pallas import tpu as pltpu
from jax.sharding import PartitionSpec as P

HEAD_DIM = 128
BLOCK_LEN = 4
MESH = pl.DeviceIdType.MESH

big_negative = -1e30


class Place:
    def __init__(self, ctx_size, vocab_size):
        self.nv = vocab_size
        self.chips = ctx_size // 2
        self.bits = [1 << i for i in range(self.chips.bit_length() - 1)]
        assert ctx_size == 2 << len(self.bits) and vocab_size % 2 == 0
        self.ctx = lax.axis_index("ctx")
        self.z = lax.axis_index("vocab")

    def flip(self, mask):
        ctx, out, bit = self.ctx, self.ctx, 1
        while bit <= mask:
            if mask & bit:
                has = lax.rem(lax.div(ctx, bit), 2)
                out = out + bit - 2 * bit * has
            bit *= 2
        return out

    def device(self, r, s, c):
        return (self.flip(2 * r + c), lax.rem(self.z + (self.nv - s) % self.nv, self.nv))

    def slot(self, r, s, c):
        return (r * self.nv + s) * 2 + c

    def onward(self, r, half):
        if r == 0:
            return list(self.bits)
        if half == 0:
            return [b for b in self.bits if b > r]
        return [b for b in self.bits if b < (r & -r)]


def entry_barrier(place):
    barrier = pltpu.get_barrier_semaphore()
    count = 0
    for r in range(place.chips):
        for s in range(place.nv):
            for c in range(2):
                if r or s or c:
                    pl.semaphore_signal(
                        barrier, inc=1, device_id=place.device(r, s, c), device_id_type=MESH
                    )
                    count += 1
    pl.semaphore_wait(barrier, count)


def up_to(value, unit):
    return (value + unit - 1) // unit * unit


def kernel(
    sizes, bq_hbm, bk_hbm, bv_hbm, doc_ref, tq_hbm, tk_hbm, tv_hbm, ts_hbm, g_ref, w_hbm, t_ref,
    bc_ref, o_ref,
    bq, kv, doc_in, c_all, c_out, c_in, tq, kcat, vcat, ts, summed,
    rows, w_ref, logits, t_col, s_out, s_in,
    in_sems, kv_send, kv_recv, d_send, d_recv, c_send, c_recv,
    w_sem, send, recv, s_send, s_recv,
):
    place = Place(*sizes)
    nv, chips = place.nv, place.chips
    tok, width = ts.shape
    cols = w_ref.shape[1]
    units = width // 128
    late = units * 5 // 48
    early = units // 2 - late
    widths = [early * 128, early * 128, late * 128, late * 128]
    per_group = nv * 2
    group = per_group * tok
    blk, part = bq.shape
    scale = 1.0 / math.sqrt(HEAD_DIM)
    heads = part // HEAD_DIM
    share = blk // nv
    pad8, pad16 = up_to(share, 8), up_to(share, 16)

    loads = [
        pltpu.make_async_copy(bk_hbm, kv.at[0, pl.ds(0, blk)], in_sems.at[0]),
        pltpu.make_async_copy(bv_hbm, kv.at[1, pl.ds(0, blk)], in_sems.at[1]),
        pltpu.make_async_copy(bq_hbm, bq, in_sems.at[2]),
        pltpu.make_async_copy(tq_hbm, tq, in_sems.at[3]),
        pltpu.make_async_copy(tk_hbm, kcat.at[pl.ds(0, tok)], in_sems.at[4]),
        pltpu.make_async_copy(tv_hbm, vcat.at[pl.ds(0, tok)], in_sems.at[5]),
        pltpu.make_async_copy(ts_hbm, ts, in_sems.at[6]),
    ]
    for load in loads:
        load.start()
    load_w = pltpu.make_async_copy(w_hbm, w_ref, w_sem)
    load_w.start()

    lane8 = lax.broadcasted_iota(jnp.int32, (8, 128), 1)
    doc_in[0] = jnp.zeros((8, 128), jnp.float32)
    doc_in[0, 0:1, 0:blk] = doc_ref[...].astype(jnp.float32)
    tiled = doc_in[0]
    span = blk
    while span < 128:
        tiled = tiled + pltpu.roll(tiled, span, 1)
        span *= 2
    doc_in[0] = tiled
    entry_barrier(place)

    kv_sent = []

    def kv_view(r, c, half):
        return kv.at[half, pl.ds((2 * r + c) * blk, blk)]

    def kv_push(src, half, dst, device):
        copy = pltpu.make_async_remote_copy(
            src_ref=kv_view(*src, half),
            dst_ref=kv_view(*dst, half),
            send_sem=kv_send.at[len(kv_sent)],
            recv_sem=kv_recv.at[2 * (2 * dst[0] + dst[1]) + half],
            device_id=device,
            device_id_type=MESH,
        )
        copy.start()
        kv_sent.append(copy)

    def kv_arrived(r, c, half):
        ref = kv_view(r, c, half)
        pltpu.make_async_copy(ref, ref, kv_recv.at[2 * (2 * r + c) + half]).wait()

    def kv_pass(r, half):
        for bit in place.onward(r, half):
            kv_push((r, 0), half, (r ^ bit, 0), place.device(bit, 0, 0))
        kv_push((r, 0), half, (r, 1), place.device(0, 0, 1))

    nearest = sorted(range(1, chips), key=lambda r: (bin(r).count("1"), r))
    for half in range(2):
        loads[half].wait()
        kv_pass(0, half)
    d_sent = []
    for r in range(chips):
        for c in range(2):
            slot = 2 * r + c
            if slot:
                copy = pltpu.make_async_remote_copy(
                    src_ref=doc_in.at[0],
                    dst_ref=doc_in.at[slot],
                    send_sem=d_send.at[slot],
                    recv_sem=d_recv.at[slot],
                    device_id=place.device(r, 0, c),
                    device_id_type=MESH,
                )
                copy.start()
                d_sent.append(copy)

    t_lane = lax.broadcasted_iota(jnp.int32, (tok, 128), 1)
    t_row = lax.broadcasted_iota(jnp.int32, (tok, 128), 0)
    in_row = 128 // tok
    for r in range(chips):
        for s in range(nv):
            for c in range(2):
                ctx, z = place.device(r, s, c)
                flat = ctx * nv + z
                line = t_ref[pl.ds(lax.div(flat, in_row), 1), :].astype(jnp.float32)
                here = t_lane == t_row + lax.rem(flat, in_row) * tok
                t_col[pl.ds(place.slot(r, s, c) * tok, tok), :] = jnp.sum(
                    jnp.where(here, line, 0.0), axis=1, keepdims=True
                )

    for r in nearest:
        for half in range(2):
            kv_arrived(r, 0, half)
            kv_pass(r, half)

    q_lane = lax.broadcasted_iota(jnp.int32, (blk, 128), 1)
    q_row = lax.broadcasted_iota(jnp.int32, (blk, 128), 0)
    own_doc = jnp.sum(jnp.where(q_lane == q_row, tiled[0:1, :], 0.0), axis=1, keepdims=True)
    own_place = q_row + place.ctx * blk
    for copy in d_sent:
        copy.wait_recv()
    masks = []
    fit = 128 // blk
    for first in range(0, 2 * chips, fit):
        docs = jnp.zeros((1, 128), jnp.float32)
        places = jnp.zeros((blk, 128), jnp.int32)
        for k in range(fit):
            slot = first + k
            mine = (q_lane >= k * blk) & (q_lane < (k + 1) * blk)
            docs = jnp.where(mine[0:1, :], doc_in[slot, 0:1, :], docs)
            places = jnp.where(mine, place.flip(slot) * blk - k * blk + q_lane, places)
        masks.append(((own_doc == docs) & (own_place >= places)).astype(jnp.float32))
    allowed = (jnp.concatenate(masks, axis=1) > 0.5)[None]
    loads[2].wait()
    for r in range(chips):
        for half in range(2):
            kv_arrived(r, 1, half)

    def softmax(scores, allowed):
        scores = jnp.where(allowed, scores * scale, big_negative)
        top = jnp.max(scores, axis=-1, keepdims=True)
        weights = jnp.where(allowed, jnp.exp(scores - top), 0.0)
        return weights.astype(jnp.bfloat16), jnp.sum(weights, axis=-1, keepdims=True)

    def dot_t(a, b):
        return lax.dot_general(a, b, (((1,), (1,)), ((), ())), preferred_element_type=jnp.float32)

    ats = [pl.ds(h * HEAD_DIM, HEAD_DIM) for h in range(heads)]
    scores = jnp.stack([dot_t(bq[:, at], kv[0, :, at]) for at in ats])
    weights, totals = softmax(scores, allowed)
    if pad8 > share:
        c_out[...] = jnp.zeros_like(c_out)
    for h, at in enumerate(ats):
        mixed = jnp.dot(weights[h], kv[1, :, at], preferred_element_type=jnp.float32) / totals[h]
        rounded = mixed.astype(jnp.bfloat16)
        bc_ref[:, at] = rounded
        c_all[:, at] = rounded.astype(jnp.float32)
    for v in range(nv):
        c_out[v, 0:share, :] = c_all[v * share:(v + 1) * share, :]

    c_sent = []
    for s in sorted(range(1, nv), key=lambda s: -min(s, nv - s)):
        device = place.device(0, s, 0)
        copy = pltpu.make_async_remote_copy(
            src_ref=c_out.at[device[1]],
            dst_ref=c_in.at[place.z],
            send_sem=c_send.at[s],
            recv_sem=c_recv.at[s],
            device_id=device,
            device_id_type=MESH,
        )
        copy.start()
        c_sent.append(copy)
    c_in[place.z] = c_out[place.z]

    deep = tok + pad16
    l_row = lax.broadcasted_iota(jnp.int32, (tok, deep), 0)
    l_col = lax.broadcasted_iota(jnp.int32, (tok, deep), 1)
    l_block = lax.div(l_row, BLOCK_LEN)
    usable = (l_col < tok) & (l_col <= l_row) & (lax.div(l_col, BLOCK_LEN) == l_block)
    usable = (usable | (l_col == tok + l_block))[None]
    for load in loads[3:]:
        load.wait()
    for copy in c_sent:
        copy.wait_recv()

    def decode(v, power):
        context = c_in[v]
        if pad16 > pad8:
            context = jnp.concatenate(
                [context, jnp.zeros((pad16 - pad8, part), jnp.float32)], axis=0
            )
        context = context.astype(jnp.bfloat16)
        start = pl.multiple_of(v * part, part)
        kcat[pl.ds(tok, pad16), pl.ds(start, part)] = context
        vcat[pl.ds(tok, pad16), pl.ds(start, part)] = context
        spots = [pl.ds(pl.multiple_of(start + h * HEAD_DIM, HEAD_DIM), HEAD_DIM) for h in range(heads)]
        scores = jnp.stack([dot_t(tq[:, at], kcat[:, at]) for at in spots])
        weights, totals = softmax(scores, usable)
        for h, at in enumerate(spots):
            mixed = jnp.dot(weights[h], vcat[:, at], preferred_element_type=jnp.float32)
            total = ts[:, at].astype(jnp.float32) + mixed / totals[h]
            summed[:, at] = total
            power = power + total * total
        return power

    power = lax.fori_loop(0, nv, decode, jnp.zeros((tok, HEAD_DIM), jnp.float32))
    power = jnp.sum(power, axis=1, keepdims=True) / width
    rows[pl.ds(0, tok), :] = (
        summed[...] * lax.rsqrt(power + 1e-05) * g_ref[...]
    ).astype(jnp.bfloat16)

    sent = []

    def view(slot, piece):
        return rows.at[pl.ds(slot * tok, tok), pl.ds(sum(widths[:piece]), widths[piece])]

    def push(src, piece, dst, device):
        dst_slot = place.slot(*dst)
        copy = pltpu.make_async_remote_copy(
            src_ref=view(place.slot(*src), piece),
            dst_ref=view(dst_slot, piece),
            send_sem=send.at[len(sent)],
            recv_sem=recv.at[4 * dst_slot + piece],
            device_id=device,
            device_id_type=MESH,
        )
        copy.start()
        sent.append(copy)

    def arrived(r, s, c, piece):
        slot = place.slot(r, s, c)
        ref = view(slot, piece)
        pltpu.make_async_copy(ref, ref, recv.at[4 * slot + piece]).wait()

    def along_vocab(r, s, piece):
        mid, half = nv // 2, piece % 2
        if s == 0:
            ahead = mid > 1 or half == 0
            back = mid > 1 or half == 1
        else:
            ahead = s < mid - 1 or (s == mid - 1 and half == 0)
            back = s > mid + 1 or (s == mid + 1 and half == 1)
        if ahead:
            push((r, s, 0), piece, (r, s + 1, 0), place.device(0, nv - 1, 0))
        if back:
            push((r, s, 0), piece, (r, (s - 1) % nv, 0), place.device(0, 1, 0))

    def along_ctx(r, s, piece):
        for bit in place.onward(r, piece % 2):
            push((r, s, 0), piece, (r ^ bit, s, 0), place.device(bit, 0, 0))

    def take(r, s, piece):
        arrived(r, s, 0, piece)
        if r == 0 or piece > 1:
            along_vocab(r, s, piece)
        if s == 0 or piece < 2:
            along_ctx(r, s, piece)
        push((r, s, 0), piece, (r, s, 1), place.device(0, 0, 1))

    order = [0]
    for d in range(1, nv // 2):
        order += [d, nv - d]
    order.append(nv // 2)

    for piece in range(2):
        along_vocab(0, 0, piece)
    for piece in (2, 3, 0, 1):
        along_ctx(0, 0, piece)
    for piece in range(2, 4):
        along_vocab(0, 0, piece)
    for piece in range(4):
        push((0, 0, 0), piece, (0, 0, 1), place.device(0, 0, 1))

    first = place.ctx * nv + place.z
    s_sent = []
    lane = lax.broadcasted_iota(jnp.int32, (128, 128), 1)
    column = lax.broadcasted_iota(jnp.int32, (128, cols), 1) + first * cols
    column = column.astype(jnp.float32)
    tile = min(256, cols)

    span_rows = max(128, tok)
    in_span = span_rows // tok

    def ready(r):
        for s in range(nv):
            for piece in range(4):
                arrived(r, s, 1, piece)

    def multiply(r):
        @pl.loop(0, cols // tile)
        def _(n):
            at = pl.ds(pl.multiple_of(n * tile, tile), tile)
            logits[:, at] = jnp.dot(
                rows[pl.ds(r * group, group), :], w_ref[:, at], preferred_element_type=jnp.float32
            )

    def reduce(r):
        @pl.loop(0, group // span_rows)
        def _(j):
            at = pl.multiple_of(j * span_rows, span_rows)
            block = logits[pl.ds(at, span_rows), :]
            top = jnp.max(block, axis=1, keepdims=True)
            mass = jnp.sum(jnp.exp(block - top), axis=1, keepdims=True)
            wanted = t_col[pl.ds(r * group + at, span_rows), :]
            pick = jnp.sum(jnp.where(column == wanted, block, 0.0), axis=1, keepdims=True)
            packed = jnp.where(lane == 0, top, jnp.where(lane == 1, mass, pick))
            turned = jnp.transpose(packed)[0:8, :]
            for k in range(in_span):
                shifted = turned if k == 0 else pltpu.roll(turned, 128 - k * tok, 1)
                s_out[r * per_group + j * in_span + k] = shifted

    def share_stats(r):
        for s in range(nv):
            for c in range(2):
                slot, there = place.slot(r, s, c), place.slot(r, (nv - s) % nv, c)
                if r or s or c:
                    copy = pltpu.make_async_remote_copy(
                        src_ref=s_out.at[slot],
                        dst_ref=s_in.at[there],
                        send_sem=s_send.at[slot],
                        recv_sem=s_recv.at[there],
                        device_id=place.device(r, s, c),
                        device_id_type=MESH,
                    )
                    copy.start()
                    s_sent.append(copy)
                else:
                    s_in[0] = s_out[0]

    outer = list(range(1, chips))
    outer.sort(key=lambda r: (bin(r).count("1"), r))
    near = [r for r in outer if r in place.bits]
    far = [r for r in outer if r not in place.bits]
    def pieces(r):
        steps = [functools.partial(multiply, r), functools.partial(reduce, r)]
        return steps + [functools.partial(share_stats, r)]

    def takes(rs, ss):
        return [(r, s, p) for r in rs for s in ss for p in (2, 3, 0, 1)]

    mids, last = order[1:-1], order[-1:]
    for event in takes(near, [0]) + takes([0], mids) + takes(far, [0]) + takes([0], last):
        take(*event)
    for event in takes(near, mids):
        take(*event)
    load_w.wait()
    ready(0)
    pending = pieces(0)
    for event in takes(near, last) + takes(far, mids):
        take(*event)
        if pending:
            pending.pop(0)()
    for step in pending:
        step()
    for r in near[:-1]:
        ready(r)
        for step in pieces(r):
            step()
    for event in takes(far, last):
        take(*event)
    for r in near[-1:] + far:
        ready(r)
        for step in pieces(r):
            step()

    for copy in s_sent:
        copy.wait_recv()
    stats = s_in[...]
    tops = stats[:, 0:1, :]
    top = jnp.max(tops, axis=0)
    mass = jnp.sum(stats[:, 1:2, :] * jnp.exp(tops - top[None]), axis=0)
    pick = jnp.sum(stats[:, 2:3, :], axis=0)
    prior = pick - (top + jnp.log(mass))
    o_ref[...] = prior[:, 0:tok]
    for copy in s_sent:
        copy.wait_send()
    for copy in sent + kv_sent + d_sent + c_sent:
        copy.wait_send()


def local(
    sizes,
    block_query,
    block_key,
    block_value,
    block_doc,
    token_query,
    token_key,
    token_value,
    token_state,
    norm_gain,
    head_weight,
    targets,
):
    ctx_size, nv = sizes
    blk, part = block_query.shape
    tok, width = token_state.shape
    cols = head_weight.shape[1]
    devices = ctx_size * nv
    tokens = devices * tok
    share = blk // nv
    pad8, pad16 = up_to(share, 8), up_to(share, 16)
    vmem = pl.BlockSpec(memory_space=pltpu.VMEM)
    hbm = pl.BlockSpec(memory_space=pl.ANY)
    dma = pltpu.SemaphoreType.DMA
    bf16, f32 = jnp.bfloat16, jnp.float32
    context, prior = pl.pallas_call(
        functools.partial(kernel, sizes),
        out_shape=(
            jax.ShapeDtypeStruct((blk, part), bf16),
            jax.ShapeDtypeStruct((1, tok), f32),
        ),
        in_specs=[hbm, hbm, hbm, vmem, hbm, hbm, hbm, hbm, vmem, hbm, vmem],
        out_specs=(vmem, vmem),
        scratch_shapes=[
            pltpu.VMEM((blk, part), bf16),
            pltpu.VMEM((2, ctx_size * blk, part), bf16),
            pltpu.VMEM((ctx_size, 8, 128), f32),
            pltpu.VMEM((blk, part), f32),
            pltpu.VMEM((nv, pad8, part), f32),
            pltpu.VMEM((nv, pad8, part), f32),
            pltpu.VMEM((tok, width), bf16),
            pltpu.VMEM((tok + pad16, width), bf16),
            pltpu.VMEM((tok + pad16, width), bf16),
            pltpu.VMEM((tok, width), bf16),
            pltpu.VMEM((tok, width), f32),
            pltpu.VMEM((tokens, width), bf16),
            pltpu.VMEM((width, cols), bf16),
            pltpu.VMEM((nv * 2 * tok, cols), f32),
            pltpu.VMEM((tokens, 1), f32),
            pltpu.VMEM((devices, 8, 128), f32),
            pltpu.VMEM((devices, 8, 128), f32),
            dma((7,)),
            dma((2 * ctx_size,)),
            dma((2 * ctx_size,)),
            dma((ctx_size,)),
            dma((ctx_size,)),
            dma((nv,)),
            dma((nv,)),
            dma,
            dma((4 * devices,)),
            dma((4 * devices,)),
            dma((devices,)),
            dma((devices,)),
        ],
        compiler_params=pltpu.CompilerParams(
            collective_id=0, has_side_effects=True, vmem_limit_bytes=60 * 1024 * 1024
        ),
        name="window",
    )(
        block_query,
        block_key,
        block_value,
        block_doc.reshape(1, blk),
        token_query,
        token_key,
        token_value,
        token_state,
        norm_gain.reshape(1, width),
        head_weight,
        targets.reshape(tokens // 128, 128),
    )
    return context, prior.reshape(tok)


def solution(mesh):
    placed = (
        P("ctx", "vocab"),
        P("ctx", "vocab"),
        P("ctx", "vocab"),
        P("ctx"),
        P(("ctx", "vocab"), None),
        P(("ctx", "vocab"), None),
        P(("ctx", "vocab"), None),
        P(("ctx", "vocab"), None),
        P(),
        P(None, ("ctx", "vocab")),
        P(),
    )
    return jax.shard_map(
        functools.partial(local, (mesh.shape["ctx"], mesh.shape["vocab"])),
        mesh=mesh,
        in_specs=placed,
        out_specs=(P("ctx", "vocab"), P(("ctx", "vocab"))),
        check_vma=False,
    )
```
